256 devices in a mesh: batch: 4 (over y_lo, core), feat: 64 (over z, x, y_hi).
Axes of the slice: x: 4, y: 4 (y_hi: 2, y_lo: 2; y = y_hi * 2 + y_lo), z: 8, core: 2. Of those that a mesh axis runs over, the one named last changes fastest.
Arguments:
- embedding: bfloat16 [512, 16384], P('batch', 'feat'), may hold values from -16 to 16
Outputs:
- embedding_grad: bfloat16 [512, 16384], P('batch', 'feat')
- cov_tiles: bfloat16 [192, 1024, 1024], P('feat', 'batch')
The draws below stay inside these ranges and needn't reach their ends.
All inputs are finite; a program needn't handle non-finite values.
Results may differ from the reference program's by a relative error of at most 0.0056.
Values may be sent and summed in bfloat16 or wider, within the bound.
No kernel may reach another device: no remote copies, remote signals or barrier semaphores. Data moves between devices by JAX's collectives and lax.ppermute only.
A program may use at most 128 MiB of HBM per device.

```python
import jax
import jax.numpy as jnp
import numpy as np
from jax import lax

F = 16384
BLK = 1024
ROWS = 512
NBLK = 16
TILES = 136
MAX_TILES = 3
SLOTS = 192
N_FEAT = 64


def draw_embedding(key, part):
    key = jax.random.fold_in(key, 5)
    key_scale, key_base = jax.random.split(key, 2)
    col_scale = jnp.exp(jax.random.uniform(key_scale, (F,), jnp.float32, jnp.log(0.3), jnp.log(2.5)))
    base = jnp.clip(jax.random.normal(key_base, (ROWS, F), jnp.float32), -5.0, 5.0)
    values = base * col_scale
    return values.astype(jnp.bfloat16)


def setup_inputs(seed: int = 0) -> dict:
    key_list = jax.random.split(jax.random.key(seed), 2)
    embedding = draw_embedding(jax.random.fold_in(key_list[1], 71), 0)
    return dict(embedding=embedding)


def reference(embedding):
    values = embedding.astype(jnp.float32)
    row_count = values.shape[0]
    col_mean = lax.optimization_barrier(jnp.sum(values, axis=0)) / row_count
    deviation = values - col_mean
    col_std = jnp.sqrt(lax.optimization_barrier(jnp.sum(deviation * deviation, axis=0)) / (row_count - 1) + 0.0001)
    var_grad = jnp.where(col_std < 1.0, -6.25 * deviation / col_std, 0.0)
    centered = deviation.astype(jnp.bfloat16)

    def column_block(block_index):
        right_cols = lax.dynamic_slice_in_dim(centered, block_index * BLK, BLK, 1)
        cov = jnp.dot(centered.T, right_cols, preferred_element_type=jnp.float32) / (row_count - 1)
        row_ids = jnp.arange(F, dtype=jnp.int32)[:, None]
        col_ids = block_index * BLK + jnp.arange(BLK, dtype=jnp.int32)[None, :]
        off_cov = jnp.where(row_ids == col_ids, 0.0, cov).astype(jnp.bfloat16)
        return jnp.dot(centered, off_cov, preferred_element_type=jnp.float32)
    pieces = lax.map(column_block, jnp.arange(NBLK, dtype=jnp.int32))
    cov_grad = jnp.transpose(pieces, (1, 0, 2)).reshape(row_count, F)
    upper_rows, upper_cols = np.triu_indices(NBLK)
    left_table = jnp.asarray(upper_rows.astype(np.int32))
    right_table = jnp.asarray(upper_cols.astype(np.int32))
    slot_ids = jnp.arange(SLOTS, dtype=jnp.int32)
    tile_ids = slot_ids // MAX_TILES + N_FEAT * (slot_ids % MAX_TILES)
    slot_valid = tile_ids < TILES
    tile_clamped = jnp.minimum(tile_ids, TILES - 1)
    left_block = left_table[tile_clamped]
    right_block = right_table[tile_clamped]
    diag_mask = jnp.arange(BLK, dtype=jnp.int32)[:, None] == jnp.arange(BLK, dtype=jnp.int32)[None, :]

    def one_tile(item):
        left_idx, right_idx, valid = item
        left_cols = lax.dynamic_slice_in_dim(centered, left_idx * BLK, BLK, 1)
        right_cols = lax.dynamic_slice_in_dim(centered, right_idx * BLK, BLK, 1)
        tile = lax.dot_general(left_cols, right_cols, (((0,), (0,)), ((), ())), preferred_element_type=jnp.float32) / (row_count - 1)
        dropped = diag_mask & (left_idx == right_idx) | jnp.logical_not(valid)
        return jnp.where(dropped, 0.0, tile).astype(jnp.bfloat16)
    cov_tiles = lax.map(one_tile, (left_block, right_block, slot_valid))
    return ((cov_grad + var_grad).astype(jnp.bfloat16), cov_tiles)
```

```python
import collections

import jax
import jax.numpy as jnp
import numpy as np
from jax import lax
from jax.sharding import Mesh
from jax.sharding import PartitionSpec as P

BLK = 1024
NBLK = 16
TILES = 136
FEATS = 64
PIECE = 256
SLOTS = 3
BATCH = ("yl", "co")
FEAT = ("z", "x", "yh")
EVERY = BATCH + FEAT


def tiles_of(f):
    upper_rows, upper_cols = np.triu_indices(NBLK)
    ids = range(f, TILES, FEATS)
    return [(int(upper_rows[t]), int(upper_cols[t])) for t in ids]


def blocks_of(f):
    found = []
    for pair in tiles_of(f):
        for j in pair:
            if j not in found:
                found.append(j)
    return found


def edge_rounds(edges):
    degree = collections.Counter()
    for s, d in edges:
        degree[("s", s)] += 1
        degree[("d", d)] += 1
    count = max(degree.values())
    taken = collections.defaultdict(dict)
    for s, d in edges:
        u, v = ("s", s), ("d", d)
        a = next(c for c in range(count) if c not in taken[u])
        b = next(c for c in range(count) if c not in taken[v])
        if a != b:
            path, node, c = [], v, a
            while c in taken[node]:
                other = taken[node][c]
                path.append((node, other, c))
                node, c = other, (b if c == a else a)
            for p, q, c in path:
                del taken[p][c]
                del taken[q][c]
            for p, q, c in path:
                o = b if c == a else a
                taken[p][o] = q
                taken[q][o] = p
        taken[u][a] = v
        taken[v][a] = u
    rounds = [[] for _ in range(count)]
    for u, row in taken.items():
        if u[0] == "s":
            for c, v in row.items():
                rounds[c].append((u[1], v[1]))
    return [sorted(r) for r in rounds]


def make_plan():
    used = collections.Counter()
    edges = []
    for f in range(FEATS):
        for j in blocks_of(f):
            for q in range(4):
                p = 4 * j + q
                if p == f:
                    continue
                y_half = q // 2
                source_half = y_half if p % 2 == f % 2 else 1 - y_half
                free = [used[(p, source_half, c)] for c in range(2)]
                core = 0 if free[0] < free[1] or (free[0] == free[1] and f % 2) else 1
                used[(p, source_half, core)] += 1
                edges.append(((source_half * 2 + core) * FEATS + p, q * FEATS + f))
    rounds = edge_rounds(edges)
    place = {}
    for r, pairs in enumerate(rounds):
        for s, d in pairs:
            place[(d, s % FEATS)] = r
    table = np.zeros((4, FEATS, 2 * SLOTS), np.int32)
    for f in range(FEATS):
        for q in range(4):
            for k, pair in enumerate(tiles_of(f)):
                for side, j in enumerate(pair):
                    p = 4 * j + q
                    table[q, f, 2 * k + side] = len(rounds) if p == f else place[(q * FEATS + f, p)]
    return rounds, table


def swap(x, axis):
    return lax.ppermute(x, axis, [(0, 1), (1, 0)])


def in_order(mine, other, index):
    first = index == 0
    return [jnp.where(first, mine, other), jnp.where(first, other, mine)]


def shards(embedding):
    local_rows, local_cols = embedding.shape
    rounds, table = make_plan()
    row_count = 4 * local_rows
    yl, co = lax.axis_index("yl"), lax.axis_index("co")
    b, f = lax.axis_index(BATCH), lax.axis_index(FEAT)
    values = lax.all_gather(embedding, BATCH, axis=0, tiled=True).astype(jnp.float32)
    col_mean = jnp.sum(values, axis=0) / row_count
    deviation = values - col_mean
    col_std = jnp.sqrt(jnp.sum(deviation * deviation, axis=0) / (row_count - 1) + 0.0001)
    centered = deviation.astype(jnp.bfloat16)
    arrived = [lax.ppermute(centered, EVERY, pairs) for pairs in rounds]

    my_deviation = lax.dynamic_slice_in_dim(deviation, b * local_rows, local_rows, 0)
    var_grad = jnp.where(col_std < 1.0, -6.25 * my_deviation / col_std, 0.0)
    mine = my_deviation.astype(jnp.bfloat16)
    gram = lax.dot_general(mine, centered, (((1,), (1,)), ((), ())), preferred_element_type=jnp.float32)
    part = lax.all_to_all(gram.reshape(8, -1, row_count), "z", 0, 0).sum(0)
    part = lax.all_to_all(jnp.broadcast_to(part, (8, *part.shape)), ("x", "yh"), 0, 0).sum(0)
    gram = lax.all_to_all(jnp.broadcast_to(part, (8, *part.shape)), "z", 0, 0).reshape(local_rows, row_count)
    gram_hi = gram.astype(jnp.bfloat16)
    gram_lo = (gram - gram_hi.astype(jnp.float32)).astype(jnp.bfloat16)
    whole = jnp.dot(gram_hi, centered, preferred_element_type=jnp.float32)
    whole = whole + jnp.dot(gram_lo, centered, preferred_element_type=jnp.float32)
    exact = centered.astype(jnp.float32)
    diagonal = jnp.sum(exact * exact, axis=0)
    cov_grad = (whole - mine.astype(jnp.float32) * diagonal) / (row_count - 1)
    grad = (cov_grad + var_grad).astype(jnp.bfloat16)

    stacked = jnp.stack([*arrived, centered])
    entry = lax.dynamic_slice(jnp.asarray(table), (b, f, 0), (1, 1, 2 * SLOTS))[0, 0]
    pieces = [lax.dynamic_index_in_dim(stacked, entry[i], 0, keepdims=False) for i in range(2 * SLOTS)]
    right = jnp.stack([pieces[1], pieces[3]])
    last = pieces[5]
    other = swap(right, "yl")
    last_other = lax.ppermute(last, ("yl", "z"), [(0, 8), (8, 0)])
    half = jnp.stack(in_order(right, other, yl))
    last_half = jnp.stack(in_order(last, last_other, yl))
    far = swap(half, "co")
    last_far = lax.ppermute(last_half, ("co", "z"), [(0, 8), (8, 0)])
    quarters = in_order(half, far, co)
    last_quarters = in_order(last_half, last_far, co)
    upper_rows, upper_cols = np.triu_indices(NBLK)
    same = np.zeros((FEATS, SLOTS), np.int32)
    for i in range(FEATS):
        for k, (left_idx, right_idx) in enumerate(tiles_of(i)):
            same[i, k] = left_idx == right_idx
    same_block = lax.dynamic_slice(jnp.asarray(same), (f, 0), (1, SLOTS))[0]
    row_ids = b * PIECE + jnp.arange(PIECE, dtype=jnp.int32)
    col_ids = jnp.arange(BLK, dtype=jnp.int32)
    on_diagonal = row_ids[:, None] == col_ids[None, :]
    tiles = []
    for k in range(SLOTS):
        if k < 2:
            ordered = [quarters[q % 2][q // 2, k] for q in range(4)]
        else:
            ordered = [last_quarters[q % 2][q // 2] for q in range(4)]
        right_cols = jnp.concatenate(ordered, axis=1)
        tile = lax.dot_general(
            pieces[2 * k], right_cols, (((0,), (0,)), ((), ())), preferred_element_type=jnp.float32
        ) / (row_count - 1)
        dropped = on_diagonal & (same_block[k] != 0)
        if k == 2:
            dropped = dropped | (f + k * FEATS >= TILES)
        tiles.append(jnp.where(dropped, 0.0, tile).astype(jnp.bfloat16))
    return grad, jnp.stack(tiles)


def solution(mesh):
    split = Mesh(mesh.devices.reshape(2, 2, 8, 4, 2), EVERY)
    in_specs = (P(BATCH, FEAT),)
    out_specs = (P(BATCH, FEAT), P(FEAT, BATCH, None))
    return jax.shard_map(shards, mesh=split, in_specs=in_specs, out_specs=out_specs, check_vma=False)
```

```python
import collections

import jax
import jax.numpy as jnp
import numpy as np
from jax import lax
from jax.experimental import pallas as pl
from jax.experimental.pallas import tpu as pltpu
from jax.sharding import Mesh
from jax.sharding import PartitionSpec as P

BLK = 1024
NBLK = 16
TILES = 136
FEATS = 64
PIECE = 256
SLOTS = 3
ENTRIES = 16
BATCH = ("yl", "co")
FEAT = ("z", "x", "yh")
EVERY = BATCH + FEAT


def tiles_of(f):
    upper_rows, upper_cols = np.triu_indices(NBLK)
    ids = range(f, TILES, FEATS)
    return [(int(upper_rows[t]), int(upper_cols[t])) for t in ids]


def blocks_of(f):
    found = []
    for pair in tiles_of(f):
        for j in pair:
            if j not in found:
                found.append(j)
    return found


def edge_rounds(edges):
    degree = collections.Counter()
    for s, d in edges:
        degree[("s", s)] += 1
        degree[("d", d)] += 1
    count = max(degree.values())
    taken = collections.defaultdict(dict)
    for s, d in edges:
        u, v = ("s", s), ("d", d)
        a = next(c for c in range(count) if c not in taken[u])
        b = next(c for c in range(count) if c not in taken[v])
        if a != b:
            path, node, c = [], v, a
            while c in taken[node]:
                other = taken[node][c]
                path.append((node, other, c))
                node, c = other, (b if c == a else a)
            for p, q, c in path:
                del taken[p][c]
                del taken[q][c]
            for p, q, c in path:
                o = b if c == a else a
                taken[p][o] = q
                taken[q][o] = p
        taken[u][a] = v
        taken[v][a] = u
    rounds = [[] for _ in range(count)]
    for u, row in taken.items():
        if u[0] == "s":
            for c, v in row.items():
                rounds[c].append((u[1], v[1]))
    return [sorted(r) for r in rounds]


def make_plan():
    used = collections.Counter()
    edges = []
    for f in range(FEATS):
        for j in blocks_of(f):
            for q in range(4):
                p = 4 * j + q
                if p == f:
                    continue
                y_half = q // 2
                source_half = y_half if p % 2 == f % 2 else 1 - y_half
                free = [used[(p, source_half, c)] for c in range(2)]
                core = 0 if free[0] < free[1] or (free[0] == free[1] and f % 2) else 1
                used[(p, source_half, core)] += 1
                edges.append(((source_half * 2 + core) * FEATS + p, q * FEATS + f))
    rounds = edge_rounds(edges)
    place = {}
    for r, pairs in enumerate(rounds):
        for s, d in pairs:
            place[(d, s % FEATS)] = r
    table = np.full((4, FEATS, ENTRIES), -1, np.int32)
    for f in range(FEATS):
        for q in range(4):
            for k, pair in enumerate(tiles_of(f)):
                for side, j in enumerate(pair):
                    p = 4 * j + q
                    table[q, f, 2 * k + side] = len(rounds) if p == f else place[(q * FEATS + f, p)]
                table[q, f, 2 * SLOTS + k] = int(pair[0] == pair[1])
    return rounds, table.reshape(-1)


def my_entries(table_ref):
    index = ((lax.axis_index("yl") * 2 + lax.axis_index("co")) * 8 + lax.axis_index("z")) * 8
    index = index + lax.axis_index("x") * 2 + lax.axis_index("yh")
    return [table_ref[index * ENTRIES + i] for i in range(3 * SLOTS)]


def fetch(entry, sources, target, sem):
    for r, source in enumerate(sources):

        @pl.when(entry == r)
        def _():
            pltpu.make_async_copy(source, target, sem).start()


def fetched(entry, source, target, sem):
    @pl.when(entry >= 0)
    def _():
        pltpu.make_async_copy(source, target, sem).wait()


def pick_kernel(table_ref, *refs):
    sources, (right_ref, last_ref, sems) = refs[:-3], refs[-3:]
    entry = my_entries(table_ref)
    targets = [right_ref.at[0], right_ref.at[1], last_ref]
    for k in range(SLOTS):
        fetch(entry[2 * k + 1], sources, targets[k], sems.at[k])
    for k in range(SLOTS):
        fetched(entry[2 * k + 1], sources[0], targets[k], sems.at[k])


def tile_kernel(scale, table_ref, *refs):
    sources, rights, lasts = refs[:-11], refs[-11:-7], refs[-7:-3]
    out_ref, left_ref, sems = refs[-3:]
    yl, co = lax.axis_index("yl"), lax.axis_index("co")
    entry = my_entries(table_ref)
    for k in range(SLOTS):
        fetch(entry[2 * k], sources, left_ref.at[k], sems.at[k])
    for k in range(SLOTS):
        fetched(entry[2 * k], sources[0], left_ref.at[k], sems.at[k])

    def fill(k, pieces):
        left = left_ref[k].T
        for n, piece in enumerate(pieces):
            q = (yl ^ (n // 2)) * 2 + (co ^ (n % 2))
            cols = pl.ds(pl.multiple_of(q * PIECE, PIECE), PIECE)
            cov = jnp.dot(left, piece[...], preferred_element_type=jnp.float32) / scale
            on_diagonal = lax.broadcasted_iota(jnp.int32, cov.shape, 0) == lax.broadcasted_iota(
                jnp.int32, cov.shape, 1
            )
            dropped = on_diagonal & (entry[2 * SLOTS + k] == 1) & (n == 0)
            out_ref[k, :, cols] = jnp.where(dropped, 0.0, cov).astype(out_ref.dtype)

    for k in range(2):
        fill(k, [piece.at[k] for piece in rights])

    @pl.when(entry[4] >= 0)
    def _():
        fill(2, lasts)

    @pl.when(entry[4] < 0)
    def _():
        out_ref[2] = jnp.zeros(out_ref.shape[1:], out_ref.dtype)


def shards(embedding):
    local_rows, local_cols = embedding.shape
    rounds, table = make_plan()
    table = jnp.asarray(table)
    row_count = 4 * local_rows
    b = lax.axis_index(BATCH)
    values = lax.all_gather(embedding, BATCH, axis=0, tiled=True).astype(jnp.float32)
    col_mean = jnp.sum(values, axis=0) / row_count
    deviation = values - col_mean
    col_std = jnp.sqrt(jnp.sum(deviation * deviation, axis=0) / (row_count - 1) + 0.0001)
    exact = lax.reduce_precision(deviation, 8, 7)
    centered = exact.astype(jnp.bfloat16)
    arrived = [lax.ppermute(centered, EVERY, pairs) for pairs in rounds]

    my_values = embedding.astype(jnp.float32)
    my_deviation = my_values - col_mean
    var_grad = jnp.where(col_std < 1.0, -6.25 * my_deviation / col_std, 0.0)
    my_exact = lax.reduce_precision(my_deviation, 8, 7)
    gram = lax.dot_general(
        my_exact.astype(jnp.bfloat16), centered, (((1,), (1,)), ((), ())), preferred_element_type=jnp.float32
    )
    part = lax.all_to_all(gram.reshape(8, -1, row_count), "z", 0, 0).sum(0)
    part = lax.all_to_all(jnp.broadcast_to(part, (8, *part.shape)), ("x", "yh"), 0, 0).sum(0)
    gram = lax.all_to_all(jnp.broadcast_to(part, (8, *part.shape)), "z", 0, 0).reshape(local_rows, row_count)
    gram_hi = lax.reduce_precision(gram, 8, 7)
    gram_lo = (gram - gram_hi).astype(jnp.bfloat16)
    whole = jnp.dot(gram_hi.astype(jnp.bfloat16), centered, preferred_element_type=jnp.float32)
    whole = whole + jnp.dot(gram_lo, centered, preferred_element_type=jnp.float32)
    diagonal = jnp.sum(exact * exact, axis=0)
    cov_grad = (whole - my_exact * diagonal) / (row_count - 1)
    grad = (cov_grad + var_grad).astype(jnp.bfloat16)

    sources = [*arrived, centered]
    anywhere = pl.BlockSpec(memory_space=pl.ANY)
    vmem = pl.BlockSpec(memory_space=pltpu.VMEM)
    smem = pl.BlockSpec(memory_space=pltpu.SMEM)
    right, last = pl.pallas_call(
        pick_kernel,
        out_shape=(
            jax.ShapeDtypeStruct((2, row_count, PIECE), jnp.bfloat16),
            jax.ShapeDtypeStruct((row_count, PIECE), jnp.bfloat16),
        ),
        in_specs=[smem] + [anywhere] * len(sources),
        out_specs=(vmem, vmem),
        scratch_shapes=[pltpu.SemaphoreType.DMA((SLOTS,))],
        compiler_params=pltpu.CompilerParams(vmem_limit_bytes=16 * 2**20),
    )(table, *sources)
    swap = [(0, 1), (1, 0)]
    swap_first = [(0, 8), (8, 0)]
    right_y = lax.ppermute(right, "yl", swap)
    right_c = lax.ppermute(right, "co", swap)
    right_yc = lax.ppermute(right_y, "co", swap)
    last_y = lax.ppermute(last, ("yl", "z"), swap_first)
    last_c = lax.ppermute(last, ("co", "z"), swap_first)
    last_yc = lax.ppermute(last_y, ("co", "z"), swap_first)
    tiles = pl.pallas_call(
        lambda *refs: tile_kernel(row_count - 1, *refs),
        out_shape=jax.ShapeDtypeStruct((SLOTS, PIECE, BLK), jnp.bfloat16),
        in_specs=[smem] + [anywhere] * len(sources) + [vmem] * 8,
        out_specs=vmem,
        scratch_shapes=[
            pltpu.VMEM((SLOTS, row_count, PIECE), jnp.bfloat16),
            pltpu.SemaphoreType.DMA((SLOTS,)),
        ],
        compiler_params=pltpu.CompilerParams(vmem_limit_bytes=32 * 2**20),
    )(table, *sources, right, right_c, right_y, right_yc, last, last_c, last_y, last_yc)
    return grad, tiles


def solution(mesh):
    split = Mesh(mesh.devices.reshape(2, 2, 8, 4, 2), EVERY)
    in_specs = (P(BATCH, FEAT),)
    out_specs = (P(BATCH, FEAT), P(FEAT, BATCH, None))
    return jax.shard_map(shards, mesh=split, in_specs=in_specs, out_specs=out_specs, check_vma=False)
```

```python
import collections

import jax
import jax.numpy as jnp
import numpy as np
from jax import lax
from jax.experimental import pallas as pl
from jax.experimental.pallas import tpu as pltpu
from jax.sharding import Mesh
from jax.sharding import PartitionSpec as P

BLK = 1024
NBLK = 16
TILES = 136
FEATS = 64
PIECE = 256
SLOTS = 3
ENTRIES = 16
BATCH = ("yl", "co")
FEAT = ("z", "x", "yh")
EVERY = BATCH + FEAT


def tiles_of(f):
    upper_rows, upper_cols = np.triu_indices(NBLK)
    ids = range(f, TILES, FEATS)
    return [(int(upper_rows[t]), int(upper_cols[t])) for t in ids]


def blocks_of(f):
    found = []
    for pair in tiles_of(f):
        for j in pair:
            if j not in found:
                found.append(j)
    return found


def edge_rounds(edges):
    degree = collections.Counter()
    for s, d in edges:
        degree[("s", s)] += 1
        degree[("d", d)] += 1
    count = max(degree.values())
    taken = collections.defaultdict(dict)
    for s, d in edges:
        u, v = ("s", s), ("d", d)
        a = next(c for c in range(count) if c not in taken[u])
        b = next(c for c in range(count) if c not in taken[v])
        if a != b:
            path, node, c = [], v, a
            while c in taken[node]:
                other = taken[node][c]
                path.append((node, other, c))
                node, c = other, (b if c == a else a)
            for p, q, c in path:
                del taken[p][c]
                del taken[q][c]
            for p, q, c in path:
                o = b if c == a else a
                taken[p][o] = q
                taken[q][o] = p
        taken[u][a] = v
        taken[v][a] = u
    rounds = [[] for _ in range(count)]
    for u, row in taken.items():
        if u[0] == "s":
            for c, v in row.items():
                rounds[c].append((u[1], v[1]))
    return [sorted(r) for r in rounds]


def make_plan():
    used = collections.Counter()
    edges = []
    for f in range(FEATS):
        for j in blocks_of(f):
            for q in range(4):
                p = 4 * j + q
                if p == f:
                    continue
                y_half = q // 2
                source_half = y_half if p % 2 == f % 2 else 1 - y_half
                free = [used[(p, source_half, c)] for c in range(2)]
                core = 0 if free[0] < free[1] or (free[0] == free[1] and f % 2) else 1
                used[(p, source_half, core)] += 1
                edges.append(((source_half * 2 + core) * FEATS + p, q * FEATS + f))
    rounds = edge_rounds(edges)
    place = {}
    for r, pairs in enumerate(rounds):
        for s, d in pairs:
            place[(d, s % FEATS)] = r
    table = np.full((4, FEATS, ENTRIES), -1, np.int32)
    for f in range(FEATS):
        for q in range(4):
            for k, pair in enumerate(tiles_of(f)):
                for side, j in enumerate(pair):
                    p = 4 * j + q
                    table[q, f, 2 * k + side] = len(rounds) if p == f else place[(q * FEATS + f, p)]
                table[q, f, 2 * SLOTS + k] = int(pair[0] == pair[1])
    return rounds, table.reshape(-1)


def my_entries(table_ref):
    index = ((lax.axis_index("yl") * 2 + lax.axis_index("co")) * 8 + lax.axis_index("z")) * 8
    index = index + lax.axis_index("x") * 2 + lax.axis_index("yh")
    return [table_ref[index * ENTRIES + i] for i in range(3 * SLOTS)]


def fetch(entry, sources, target, sem):
    for r, source in enumerate(sources):

        @pl.when(entry == r)
        def _():
            pltpu.make_async_copy(source, target, sem).start()


def fetched(entry, source, target, sem):
    @pl.when(entry >= 0)
    def _():
        pltpu.make_async_copy(source, target, sem).wait()


def pick_kernel(table_ref, *refs):
    sources, (right_ref, sems) = refs[:-2], refs[-2:]
    entry = my_entries(table_ref)
    targets = [right_ref.at[k] for k in range(SLOTS)]
    for k in range(SLOTS):
        fetch(entry[2 * k + 1], sources, targets[k], sems.at[k])
    for k in range(SLOTS):
        fetched(entry[2 * k + 1], sources[0], targets[k], sems.at[k])


def tile_kernel(scale, table_ref, *refs):
    sources, rights, lasts = refs[:-9], refs[-9:-5], refs[-5:-3]
    out_ref, left_ref, sems = refs[-3:]
    yl, co = lax.axis_index("yl"), lax.axis_index("co")
    entry = my_entries(table_ref)
    for k in range(SLOTS):
        fetch(entry[2 * k], sources, left_ref.at[k], sems.at[k])
    for k in range(SLOTS):
        fetched(entry[2 * k], sources[0], left_ref.at[k], sems.at[k])

    def fill(k, pieces):
        left = left_ref[k].T
        for n, piece in enumerate(pieces):
            q = (yl ^ (n // 2)) * 2 + (co ^ (n % 2))
            cols = pl.ds(pl.multiple_of(q * PIECE, PIECE), PIECE)
            cov = jnp.dot(left, piece[...], preferred_element_type=jnp.float32) / scale
            on_diagonal = lax.broadcasted_iota(jnp.int32, cov.shape, 0) == lax.broadcasted_iota(
                jnp.int32, cov.shape, 1
            )
            dropped = on_diagonal & (entry[2 * SLOTS + k] == 1) & (n == 0)
            out_ref[k, :, cols] = jnp.where(dropped, 0.0, cov).astype(out_ref.dtype)

    for k in range(2):
        fill(k, [piece.at[k] for piece in rights])

    @pl.when(entry[4] >= 0)
    def _():
        fill(2, [rights[0].at[2], rights[1].at[2], *lasts])

    @pl.when(entry[4] < 0)
    def _():
        out_ref[2] = jnp.zeros(out_ref.shape[1:], out_ref.dtype)


def shards(embedding):
    local_rows, local_cols = embedding.shape
    rounds, table = make_plan()
    table = jnp.asarray(table)
    row_count = 4 * local_rows
    b = lax.axis_index(BATCH)
    values = lax.all_gather(embedding, BATCH, axis=0, tiled=True).astype(jnp.float32)
    col_mean = jnp.sum(values, axis=0) / row_count
    deviation = values - col_mean
    col_std = jnp.sqrt(jnp.sum(deviation * deviation, axis=0) / (row_count - 1) + 0.0001)
    exact = lax.reduce_precision(deviation, 8, 7)
    centered = exact.astype(jnp.bfloat16)
    arrived = [lax.ppermute(centered, EVERY, pairs) for pairs in rounds]

    my_values = embedding.astype(jnp.float32)
    my_deviation = my_values - col_mean
    var_grad = jnp.where(col_std < 1.0, -6.25 * my_deviation / col_std, 0.0)
    my_exact = lax.reduce_precision(my_deviation, 8, 7)
    gram = lax.dot_general(
        my_exact.astype(jnp.bfloat16), centered, (((1,), (1,)), ((), ())), preferred_element_type=jnp.float32
    )
    part = lax.all_to_all(gram.reshape(8, -1, row_count), ("x", "yh"), 0, 0).sum(0)
    part = lax.all_to_all(jnp.broadcast_to(part, (8, *part.shape)), "z", 0, 0).sum(0)
    gram = lax.all_to_all(jnp.broadcast_to(part, (8, *part.shape)), ("x", "yh"), 0, 0).reshape(local_rows, row_count)
    gram_hi = lax.reduce_precision(gram, 8, 7)
    gram_lo = (gram - gram_hi).astype(jnp.bfloat16)
    whole = jnp.dot(gram_hi.astype(jnp.bfloat16), centered, preferred_element_type=jnp.float32)
    whole = whole + jnp.dot(gram_lo, centered, preferred_element_type=jnp.float32)
    diagonal = jnp.sum(exact * exact, axis=0)
    cov_grad = (whole - my_exact * diagonal) / (row_count - 1)
    grad = (cov_grad + var_grad).astype(jnp.bfloat16)

    sources = [*arrived, centered]
    anywhere = pl.BlockSpec(memory_space=pl.ANY)
    vmem = pl.BlockSpec(memory_space=pltpu.VMEM)
    smem = pl.BlockSpec(memory_space=pltpu.SMEM)
    swap = [(0, 1), (1, 0)]
    swap_first = [(0, 8), (8, 0)]
    right = pl.pallas_call(
        pick_kernel,
        out_shape=jax.ShapeDtypeStruct((3, row_count, PIECE), jnp.bfloat16),
        in_specs=[smem] + [anywhere] * len(sources),
        out_specs=vmem,
        scratch_shapes=[pltpu.SemaphoreType.DMA((SLOTS,))],
        compiler_params=pltpu.CompilerParams(vmem_limit_bytes=16 * 2**20),
    )(table, *sources)
    right_y = lax.ppermute(right[:2], "yl", swap)
    last_y = lax.ppermute(right[2], ("yl", "z"), swap_first)
    right_c = lax.ppermute(right, "co", swap)
    right_yc = lax.ppermute(right_y, "co", swap)
    last_yc = lax.ppermute(last_y, ("co", "z"), swap_first)
    tiles = pl.pallas_call(
        lambda *refs: tile_kernel(row_count - 1, *refs),
        out_shape=jax.ShapeDtypeStruct((SLOTS, PIECE, BLK), jnp.bfloat16),
        in_specs=[smem] + [anywhere] * len(sources) + [vmem] * 6,
        out_specs=vmem,
        scratch_shapes=[
            pltpu.VMEM((SLOTS, row_count, PIECE), jnp.bfloat16),
            pltpu.SemaphoreType.DMA((SLOTS,)),
        ],
        compiler_params=pltpu.CompilerParams(vmem_limit_bytes=32 * 2**20),
    )(table, *sources, right, right_c, right_y, right_yc, last_y, last_yc)
    return grad, tiles


def solution(mesh):
    split = Mesh(mesh.devices.reshape(2, 2, 8, 4, 2), EVERY)
    in_specs = (P(BATCH, FEAT),)
    out_specs = (P(BATCH, FEAT), P(FEAT, BATCH, None))
    return jax.shard_map(shards, mesh=split, in_specs=in_specs, out_specs=out_specs, check_vma=False)
```

```python
import collections

import jax
import jax.numpy as jnp
import numpy as np
from jax import lax
from jax.experimental import pallas as pl
from jax.experimental.pallas import tpu as pltpu
from jax.sharding import Mesh
from jax.sharding import PartitionSpec as P

BLK = 1024
NBLK = 16
TILES = 136
FEATS = 64
PIECE = 256
SLOTS = 3
ENTRIES = 16
BATCH = ("yl", "co")
FEAT = ("z", "x", "yh")
EVERY = BATCH + FEAT


def tiles_of(f):
    upper_rows, upper_cols = np.triu_indices(NBLK)
    ids = range(f, TILES, FEATS)
    return [(int(upper_rows[t]), int(upper_cols[t])) for t in ids]


def blocks_of(f):
    found = []
    for pair in tiles_of(f):
        for j in pair:
            if j not in found:
                found.append(j)
    return found


def edge_rounds(edges):
    degree = collections.Counter()
    for s, d in edges:
        degree[("s", s)] += 1
        degree[("d", d)] += 1
    count = max(degree.values())
    taken = collections.defaultdict(dict)
    for s, d in edges:
        u, v = ("s", s), ("d", d)
        a = next(c for c in range(count) if c not in taken[u])
        b = next(c for c in range(count) if c not in taken[v])
        if a != b:
            path, node, c = [], v, a
            while c in taken[node]:
                other = taken[node][c]
                path.append((node, other, c))
                node, c = other, (b if c == a else a)
            for p, q, c in path:
                del taken[p][c]
                del taken[q][c]
            for p, q, c in path:
                o = b if c == a else a
                taken[p][o] = q
                taken[q][o] = p
        taken[u][a] = v
        taken[v][a] = u
    rounds = [[] for _ in range(count)]
    for u, row in taken.items():
        if u[0] == "s":
            for c, v in row.items():
                rounds[c].append((u[1], v[1]))
    return [sorted(r) for r in rounds]


def make_plan():
    used = collections.Counter()
    edges = []
    for f in range(FEATS):
        for j in blocks_of(f):
            for q in range(4):
                p = 4 * j + q
                if p == f:
                    continue
                y_half = q // 2
                source_half = y_half if p % 2 == f % 2 else 1 - y_half
                free = [used[(p, source_half, c)] for c in range(2)]
                core = 0 if free[0] < free[1] or (free[0] == free[1] and f % 2) else 1
                used[(p, source_half, core)] += 1
                edges.append(((source_half * 2 + core) * FEATS + p, q * FEATS + f))
    rounds = edge_rounds(edges)
    place = {}
    for r, pairs in enumerate(rounds):
        for s, d in pairs:
            place[(d, s % FEATS)] = r
    table = np.full((4, FEATS, ENTRIES), -1, np.int32)
    for f in range(FEATS):
        for q in range(4):
            for k, pair in enumerate(tiles_of(f)):
                for side, j in enumerate(pair):
                    p = 4 * j + q
                    table[q, f, 2 * k + side] = len(rounds) if p == f else place[(q * FEATS + f, p)]
                table[q, f, 2 * SLOTS + k] = int(pair[0] == pair[1])
    return rounds, table.reshape(-1)


def my_entries(table_ref):
    index = ((lax.axis_index("yl") * 2 + lax.axis_index("co")) * 8 + lax.axis_index("z")) * 8
    index = index + lax.axis_index("x") * 2 + lax.axis_index("yh")
    return [table_ref[index * ENTRIES + i] for i in range(3 * SLOTS)]


def fetch(entry, sources, target, sem):
    for r, source in enumerate(sources):

        @pl.when(entry == r)
        def _():
            pltpu.make_async_copy(source, target, sem).start()


def fetched(entry, source, target, sem):
    @pl.when(entry >= 0)
    def _():
        pltpu.make_async_copy(source, target, sem).wait()


def pick_kernel(table_ref, *refs):
    sources, (right_ref, pair_ref, last_ref, sems) = refs[:-4], refs[-4:]
    entry = my_entries(table_ref)
    jobs = [(1, pair_ref.at[0]), (3, pair_ref.at[1]), (5, last_ref)]
    jobs += [(2 * k + 1, right_ref.at[k]) for k in range(SLOTS)]
    for i, (e, target) in enumerate(jobs):
        fetch(entry[e], sources, target, sems.at[i])
    for i, (e, target) in enumerate(jobs):
        fetched(entry[e], sources[0], target, sems.at[i])


def tile_kernel(scale, table_ref, *refs):
    sources, rights, lasts = refs[:-11], refs[-11:-7], refs[-7:-5]
    out_ref, left_ref, tile_ref, sems, out_sems = refs[-5:]
    yl, co = lax.axis_index("yl"), lax.axis_index("co")
    entry = my_entries(table_ref)
    for k in range(SLOTS):
        fetch(entry[2 * k], sources, left_ref.at[k], sems.at[k])

    def send(k):
        return pltpu.make_async_copy(tile_ref.at[k], out_ref.at[k], out_sems.at[k])

    @pl.when(entry[4] < 0)
    def _():
        tile_ref[2] = jnp.zeros(tile_ref.shape[1:], tile_ref.dtype)
        send(2).start()

    def fill(k, pieces):
        fetched(entry[2 * k], sources[0], left_ref.at[k], sems.at[k])
        left = left_ref[k].T
        for n, piece in enumerate(pieces):
            q = (yl ^ (n // 2)) * 2 + (co ^ (n % 2))
            cols = pl.ds(pl.multiple_of(q * PIECE, PIECE), PIECE)
            cov = jnp.dot(left, piece[...], preferred_element_type=jnp.float32) * (1.0 / scale)
            on_diagonal = lax.broadcasted_iota(jnp.int32, cov.shape, 0) == lax.broadcasted_iota(
                jnp.int32, cov.shape, 1
            )
            dropped = on_diagonal & (entry[2 * SLOTS + k] == 1) & (n == 0)
            tile_ref[k, :, cols] = jnp.where(dropped, 0.0, cov).astype(tile_ref.dtype)
        send(k).start()

    for k in range(2):
        fill(k, [piece.at[k] for piece in rights])

    @pl.when(entry[4] >= 0)
    def _():
        fill(2, [rights[0].at[2], rights[1].at[2], *lasts])

    for k in range(SLOTS):
        send(k).wait()


def shards(embedding):
    local_rows, local_cols = embedding.shape
    rounds, table = make_plan()
    table = jnp.asarray(table)
    row_count = 4 * local_rows
    b = lax.axis_index(BATCH)
    values = lax.all_gather(embedding, BATCH, axis=0, tiled=True).astype(jnp.float32)
    col_mean = jnp.sum(values, axis=0) / row_count
    deviation = values - col_mean
    col_std = jnp.sqrt(jnp.sum(deviation * deviation, axis=0) / (row_count - 1) + 0.0001)
    exact = lax.reduce_precision(deviation, 8, 7)
    centered = exact.astype(jnp.bfloat16)
    arrived = [lax.ppermute(centered, EVERY, pairs) for pairs in rounds]

    my_values = embedding.astype(jnp.float32)
    my_deviation = my_values - col_mean
    var_grad = jnp.where(col_std < 1.0, -6.25 * my_deviation / col_std, 0.0)
    my_exact = lax.reduce_precision(my_deviation, 8, 7)
    gram = lax.dot_general(
        my_exact.astype(jnp.bfloat16), centered, (((1,), (1,)), ((), ())), preferred_element_type=jnp.float32
    )
    part = lax.all_to_all(gram.reshape(8, -1, row_count), ("x", "yh"), 0, 0).sum(0)
    part = part.astype(jnp.bfloat16)
    part = lax.all_to_all(jnp.broadcast_to(part, (8, *part.shape)), "z", 0, 0).astype(jnp.float32).sum(0)
    gram = lax.all_to_all(jnp.broadcast_to(part, (8, *part.shape)), ("x", "yh"), 0, 0).reshape(local_rows, row_count)
    gram_hi = lax.reduce_precision(gram, 8, 7)
    gram_lo = (gram - gram_hi).astype(jnp.bfloat16)
    whole = jnp.dot(gram_hi.astype(jnp.bfloat16), centered, preferred_element_type=jnp.float32)
    whole = whole + jnp.dot(gram_lo, centered, preferred_element_type=jnp.float32)
    diagonal = jnp.sum(exact * exact, axis=0)
    cov_grad = (whole - my_exact * diagonal) / (row_count - 1)
    grad = (cov_grad + var_grad).astype(jnp.bfloat16)

    sources = [*arrived, centered]
    anywhere = pl.BlockSpec(memory_space=pl.ANY)
    vmem = pl.BlockSpec(memory_space=pltpu.VMEM)
    smem = pl.BlockSpec(memory_space=pltpu.SMEM)
    swap = [(0, 1), (1, 0)]
    swap_first = [(0, 8), (8, 0)]
    right, pair, last = pl.pallas_call(
        pick_kernel,
        out_shape=[
            jax.ShapeDtypeStruct((3, row_count, PIECE), jnp.bfloat16),
            jax.ShapeDtypeStruct((2, row_count, PIECE), jnp.bfloat16),
            jax.ShapeDtypeStruct((row_count, PIECE), jnp.bfloat16),
        ],
        in_specs=[smem] + [anywhere] * len(sources),
        out_specs=[vmem] * 3,
        scratch_shapes=[pltpu.SemaphoreType.DMA((2 * SLOTS,))],
        compiler_params=pltpu.CompilerParams(vmem_limit_bytes=16 * 2**20),
    )(table, *sources)
    right_y = lax.ppermute(pair, "yl", swap)
    last_y = lax.ppermute(last, ("yl", "z"), swap_first)
    right_c = lax.ppermute(right, "co", swap)
    right_yc = lax.ppermute(right_y, "co", swap)
    last_yc = lax.ppermute(last_y, ("co", "z"), swap_first)
    tiles = pl.pallas_call(
        lambda *refs: tile_kernel(row_count - 1, *refs),
        out_shape=jax.ShapeDtypeStruct((SLOTS, PIECE, BLK), jnp.bfloat16),
        in_specs=[smem] + [anywhere] * len(sources) + [vmem] * 6,
        out_specs=anywhere,
        scratch_shapes=[
            pltpu.VMEM((SLOTS, row_count, PIECE), jnp.bfloat16),
            pltpu.VMEM((SLOTS, PIECE, BLK), jnp.bfloat16),
            pltpu.SemaphoreType.DMA((SLOTS,)),
            pltpu.SemaphoreType.DMA((SLOTS,)),
        ],
        compiler_params=pltpu.CompilerParams(vmem_limit_bytes=32 * 2**20),
    )(table, *sources, right, right_c, right_y, right_yc, last_y, last_yc)
    return grad, tiles


def solution(mesh):
    split = Mesh(mesh.devices.reshape(2, 2, 8, 4, 2), EVERY)
    in_specs = (P(BATCH, FEAT),)
    out_specs = (P(BATCH, FEAT), P(FEAT, BATCH, None))
    return jax.shard_map(shards, mesh=split, in_specs=in_specs, out_specs=out_specs, check_vma=False)
```
